32 devices in a mesh: row: 8 (over z, y), col: 4 (over x, core).
Axes of the slice: x: 2, y: 2, z: 4, core: 2. Of those that a mesh axis runs over, the one named last changes fastest.
Arguments:
- acc_feats: float32 [16384, 512], P(('row', 'col')), may hold values from -6 to 6
- content_feats: float32 [8192, 512], P('col', 'row'), may hold values from -6 to 6
- block_values: float32 [8, 4, 128, 128, 128], P('row', 'col'), may hold values from 0.02 to 1
- block_rows: int32 [8, 4, 128], P('row', 'col'), may hold values from 0 to 15, as said below
- block_cols: int32 [8, 4, 128], P('row', 'col'), may hold values from 0 to 15, as said below
- block_count: int32 [8, 4], P('row', 'col'), may hold values from 16 to 128, as said below
- w_self: float32 [512, 512], replicated, may hold values from -0.25 to 0.25
- w_neigh: float32 [512, 512], replicated, may hold values from -0.25 to 0.25
- out_grad: float32 [16384, 512], P(('row', 'col')), may hold values from -6 to 6
Outputs:
- layer_out: float32 [16384, 512], P(('row', 'col'))
- grad_acc: float32 [16384, 512], P(('row', 'col'))
- grad_content: float32 [8192, 512], P('col', 'row')
- grad_self: float32 [512, 512], replicated
- grad_neigh: float32 [512, 512], replicated
The draws below stay inside these ranges and needn't reach their ends.
Inputs may be any that keep to these rules, and one draw needn't show every extreme that they name: `block_count`: exactly one device has 128 live slots; every other device has between 16 and 64. `block_rows`: the slots of one device hold distinct (block row, block column) positions; slots at or beyond the device's count are not part of the adjacency. `block_cols`: see block_rows.
All inputs are finite; a program needn't handle non-finite values.
Results may differ from the reference program's by a relative error of at most 0.0003.
Values sent between devices are 32-bit elements; how exact they have to be, the bound alone decides.
A program may use at most 128 MiB of HBM per device.

```python
import math
import jax
import jax.numpy as jnp
from jax import lax

F = 512
BLK = 128
BR = 16
BC = 16
CAP = 128
ACC = 16384
CONTENT = 8192
N_ROW = 8
N_COL = 4


def block_layout(key):
    sub_key = jax.random.fold_in(key, 7)
    device_keys = jax.random.split(sub_key, N_ROW * N_COL)

    def one_device(device_key):
        return jax.random.permutation(device_key, BR * BC)[:CAP]
    places = jax.vmap(one_device)(device_keys)
    return places.reshape(N_ROW, N_COL, CAP).astype(jnp.int32)


def draw_block_rows(key, part):
    return block_layout(key) // BC


def draw_block_cols(key, part):
    return block_layout(key) % BC


def draw_block_count(key, part):
    lowest = max(1, CAP // 8)
    upper_bound = max(lowest + 1, CAP // 2 + 1)
    counts = jax.random.randint(jax.random.fold_in(key, 11), (N_ROW * N_COL,), lowest, upper_bound, dtype=jnp.int32)
    busiest = jax.random.randint(jax.random.fold_in(key, 12), (), 0, N_ROW * N_COL, dtype=jnp.int32)
    counts = jnp.where(jnp.arange(N_ROW * N_COL, dtype=jnp.int32) == busiest, CAP, counts)
    return counts.reshape(N_ROW, N_COL).astype(jnp.int32)


def level_of(stream_key, extent, shards, least, high):
    level = 1.0
    for position, blocks in shards:
        heights = jax.random.uniform(jax.random.fold_in(jax.random.fold_in(stream_key, 6), position), (blocks,), jnp.float32, least / len(shards), high / len(shards))
        level = level * jnp.repeat(jnp.exp(heights), extent[position] // blocks).reshape((-1,) + (1,) * (len(extent) - 1 - position))
    return level


def normal_values(rng, extent, deviation, most, cuts=(), kind=jnp.bfloat16):
    entries = jax.random.normal(rng, extent, jnp.float32) * deviation
    if len(cuts) > 0:
        entries = level_of(rng, extent, cuts, -0.22, 0.18) * entries
    return jnp.clip(entries, min=-most, max=most).astype(kind)


def setup_inputs(seed: int = 0) -> dict:
    seeds = jax.random.split(jax.random.key(seed), 10)
    acc_feats = normal_values(seeds[0], (ACC, F), 1.0, 6.0, ((0, 32),), jnp.float32)
    content_feats = normal_values(seeds[1], (CONTENT, F), 1.0, 6.0, ((0, 4), (1, 8)), jnp.float32)
    block_values = jnp.clip(jnp.exp(math.log(1.0) - 3.912023 * jax.random.uniform(seeds[2], (N_ROW, N_COL, CAP, BLK, BLK), jnp.float32) ** level_of(seeds[2], (N_ROW, N_COL, CAP, BLK, BLK), ((0, 8), (1, 4)), -0.2, 0.2)), 0.02, 1.0)
    block_rows = draw_block_rows(jax.random.fold_in(seeds[9], 71), 0)
    block_cols = draw_block_cols(jax.random.fold_in(seeds[9], 71), 0)
    block_count = draw_block_count(jax.random.fold_in(seeds[9], 71), 0)
    w_self = normal_values(seeds[6], (F, F), F ** -0.5, 0.25, (), jnp.float32)
    w_neigh = normal_values(seeds[7], (F, F), F ** -0.5, 0.25, (), jnp.float32)
    out_grad = normal_values(seeds[8], (ACC, F), 1.0, 6.0, ((0, 32),), jnp.float32)
    return {"acc_feats": acc_feats, "content_feats": content_feats, "block_values": block_values, "block_rows": block_rows, "block_cols": block_cols, "block_count": block_count, "w_self": w_self, "w_neigh": w_neigh, "out_grad": out_grad}


highest = lax.Precision.HIGHEST
rms_epsilon = 1e-05

def tile_forward(block_vals, row_ids, col_ids, live_count, source):
    channels = source.shape[1]
    picked = source.reshape(BC, BLK, channels)[col_ids]
    products = jnp.einsum('kij,kjw->kiw', block_vals, picked, precision=highest)
    is_live = jnp.arange(block_vals.shape[0], dtype=jnp.int32) < live_count
    one_hot = ((row_ids[None, :] == jnp.arange(BR, dtype=jnp.int32)[:, None]) & is_live[None, :]).astype(jnp.float32)
    return jnp.einsum('rk,kiw->riw', one_hot, products, precision=highest).reshape(BR * BLK, channels)

def tile_backward(block_vals, row_ids, col_ids, live_count, grad_rows):
    channels = grad_rows.shape[1]
    picked = grad_rows.reshape(BR, BLK, channels)[row_ids]
    products = jnp.einsum('kij,kiw->kjw', block_vals, picked, precision=highest)
    is_live = jnp.arange(block_vals.shape[0], dtype=jnp.int32) < live_count
    one_hot = ((col_ids[None, :] == jnp.arange(BC, dtype=jnp.int32)[:, None]) & is_live[None, :]).astype(jnp.float32)
    return jnp.einsum('ck,kjw->cjw', one_hot, products, precision=highest).reshape(BC * BLK, channels)

def tile_degree(block_vals, row_ids, live_count):
    row_sums = lax.optimization_barrier(jnp.sum(block_vals, axis=2))
    is_live = jnp.arange(block_vals.shape[0], dtype=jnp.int32) < live_count
    one_hot = ((row_ids[None, :] == jnp.arange(BR, dtype=jnp.int32)[:, None]) & is_live[None, :]).astype(jnp.float32)
    return jnp.dot(one_hot, row_sums, precision=highest).reshape(BR * BLK)

def reference(acc_feats, content_feats, block_values, block_rows, block_cols, block_count, w_self, w_neigh, out_grad):
    content_split = content_feats.reshape(N_COL, BC * BLK, F)
    col_range = jnp.arange(N_COL, dtype=jnp.int32)
    row_range = jnp.arange(N_ROW, dtype=jnp.int32)

    def row_shard(row_index):

        def add_column(running, col_index):
            own_values = block_values[row_index, col_index]
            own_rows = block_rows[row_index, col_index]
            own_cols = block_cols[row_index, col_index]
            own_count = block_count[row_index, col_index]
            new_sums = running[0] + tile_forward(own_values, own_rows, own_cols, own_count, content_split[col_index])
            new_degree = running[1] + tile_degree(own_values, own_rows, own_count)
            return ((new_sums, new_degree), None)
        start_value = (jnp.zeros((BR * BLK, F), jnp.float32), jnp.zeros((BR * BLK,), jnp.float32))
        result, _ = lax.scan(add_column, start_value, col_range)
        return result
    summed, degree = lax.map(row_shard, row_range)
    summed = summed.reshape(ACC, F)
    degree = degree.reshape(ACC)
    inv_degree = lax.rsqrt(1.0 + degree)[:, None]
    neigh = summed * inv_degree
    pre_act = jnp.dot(acc_feats, w_self, precision=highest) + jnp.dot(neigh, w_neigh, precision=highest)
    sigmoid_pre = jax.nn.sigmoid(pre_act)
    activation = pre_act * sigmoid_pre
    inv_rms = lax.rsqrt(lax.optimization_barrier(jnp.mean(activation * activation, axis=1, keepdims=True)) + rms_epsilon)
    layer_out = activation * inv_rms
    d_act = (out_grad - layer_out * lax.optimization_barrier(jnp.mean(out_grad * layer_out, axis=1, keepdims=True))) * inv_rms
    d_pre = d_act * sigmoid_pre * (1.0 + pre_act * (1.0 - sigmoid_pre))
    grad_acc = jnp.dot(d_pre, w_self.T, precision=highest)
    d_gathered = jnp.dot(d_pre, w_neigh.T, precision=highest) * inv_degree
    grad_split = d_gathered.reshape(N_ROW, BR * BLK, F)

    def col_shard(col_index):

        def add_row(running, row_index):
            term = tile_backward(block_values[row_index, col_index], block_rows[row_index, col_index], block_cols[row_index, col_index], block_count[row_index, col_index], grad_split[row_index])
            return (running + term, None)
        result, _ = lax.scan(add_row, jnp.zeros((BC * BLK, F), jnp.float32), row_range)
        return result
    grad_content = lax.map(col_shard, col_range).reshape(CONTENT, F)
    norm_factor = 1.0 / math.sqrt(ACC)
    grad_self = jnp.dot(acc_feats.T, d_pre, precision=highest) * norm_factor
    grad_neigh = jnp.dot(neigh.T, d_pre, precision=highest) * norm_factor
    return (layer_out, grad_acc, grad_content, grad_self, grad_neigh)
```

```python
import functools
import math

import jax
import jax.numpy as jnp
from jax import lax
from jax.experimental import pallas as pl
from jax.experimental.pallas import tpu as pltpu
from jax.sharding import PartitionSpec as P

BLK = 128
BR = 16
BC = 16
GROUP = 8
PAD = 8
VMEM_LIMIT = 48 * 1024 * 1024
high = lax.Precision.HIGH
rms_epsilon = 1e-05


def split(x):
    hi = x.astype(jnp.bfloat16)
    lo = (x - hi.astype(jnp.float32)).astype(jnp.bfloat16)
    return hi, lo


def forward_kernel(per_chunk, rows_ref, cols_ref, count_ref, vals_ref, source_ref, out_ref, xs, degs):
    step = pl.program_id(0)
    chunks, chunk_rows, _ = out_ref.shape

    @pl.when(step == 0)
    def _():
        for block in range(BC):
            hi, lo = split(source_ref[:, block * BLK : (block + 1) * BLK].T)
            xs[block, 0:BLK, :] = hi
            xs[block, BLK:, :] = lo
        out_ref[...] = jnp.zeros_like(out_ref)
        degs[...] = jnp.zeros_like(degs)

    ones = jnp.ones((8, 2 * BLK), jnp.bfloat16)
    for k in range(GROUP):
        slot = step * GROUP + k

        @pl.when(slot < count_ref[0])
        def _():
            row, col = rows_ref[slot], cols_ref[slot]
            hi, lo = split(vals_ref[k])
            left = jnp.concatenate(
                [jnp.concatenate([hi, hi], axis=1), jnp.concatenate([lo, lo], axis=1)], axis=0
            )
            product = jnp.dot(left, xs[col], preferred_element_type=jnp.float32)
            chunk = row // per_chunk
            begin = pl.multiple_of((row - chunk * per_chunk) * BLK, BLK)
            out_ref[chunk, pl.ds(begin, BLK), :] += product[:BLK] + product[BLK:]
            degs[row] += lax.dot_general(
                ones,
                jnp.concatenate([hi, lo], axis=1),
                (((1,), (1,)), ((), ())),
                preferred_element_type=jnp.float32,
            )

    @pl.when(step == pl.num_programs(0) - 1)
    def _():
        for row in range(BR):
            chunk, place = row // per_chunk, row % per_chunk
            out_ref[chunk, chunk_rows - PAD :, place * BLK : (place + 1) * BLK] = degs[row]


def backward_kernel(rows_ref, cols_ref, count_ref, vals_ref, grad_ref, out_ref, gs):
    step = pl.program_id(0)

    @pl.when(step == 0)
    def _():
        for block in range(BR):
            hi, lo = split(grad_ref[block * BLK : (block + 1) * BLK, :].T)
            gs[block, :, 0:BLK] = hi
            gs[block, :, BLK:] = lo
        out_ref[...] = jnp.zeros_like(out_ref)

    for k in range(GROUP):
        slot = step * GROUP + k

        @pl.when(slot < count_ref[0])
        def _():
            row, col = rows_ref[slot], cols_ref[slot]
            hi, lo = split(vals_ref[k])
            both = jnp.concatenate([hi, lo], axis=1)
            right = jnp.concatenate([both, both], axis=0)
            product = jnp.dot(gs[row], right, preferred_element_type=jnp.float32)
            begin = pl.multiple_of(col * BLK, BLK)
            out_ref[:, pl.ds(begin, BLK)] += product[:, :BLK] + product[:, BLK:]


def values_index(step, rows_ref, cols_ref, count_ref):
    return (jnp.minimum(step, (count_ref[0] - 1) // GROUP), 0, 0)


def whole(*shape):
    return pl.BlockSpec(shape, lambda step, *_: (0,) * len(shape))


def forward_tiles(vals, rows, cols, count, source, chunks):
    channels = source.shape[0]
    per_chunk = BR // chunks
    chunk_rows = per_chunk * BLK + PAD
    slots = vals.shape[0]
    return pl.pallas_call(
        functools.partial(forward_kernel, per_chunk),
        out_shape=jax.ShapeDtypeStruct((chunks, chunk_rows, channels), jnp.float32),
        grid_spec=pltpu.PrefetchScalarGridSpec(
            num_scalar_prefetch=3,
            grid=(slots // GROUP,),
            in_specs=[
                pl.BlockSpec((GROUP, BLK, BLK), values_index),
                whole(channels, BC * BLK),
            ],
            out_specs=whole(chunks, chunk_rows, channels),
            scratch_shapes=[
                pltpu.VMEM((BC, 2 * BLK, channels), jnp.bfloat16),
                pltpu.VMEM((BR, 8, BLK), jnp.float32),
            ],
        ),
        compiler_params=pltpu.CompilerParams(vmem_limit_bytes=VMEM_LIMIT),
        cost_estimate=pl.CostEstimate(
            flops=slots * BLK * BLK * channels * 4, bytes_accessed=16_000_000, transcendentals=0
        ),
    )(rows, cols, count, vals, source)


def backward_tiles(vals, rows, cols, count, grad_rows):
    channels = grad_rows.shape[1]
    slots = vals.shape[0]
    return pl.pallas_call(
        backward_kernel,
        out_shape=jax.ShapeDtypeStruct((channels, BC * BLK), jnp.float32),
        grid_spec=pltpu.PrefetchScalarGridSpec(
            num_scalar_prefetch=3,
            grid=(slots // GROUP,),
            in_specs=[
                pl.BlockSpec((GROUP, BLK, BLK), values_index),
                whole(BR * BLK, channels),
            ],
            out_specs=whole(channels, BC * BLK),
            scratch_shapes=[pltpu.VMEM((BR, channels, 2 * BLK), jnp.bfloat16)],
        ),
        compiler_params=pltpu.CompilerParams(vmem_limit_bytes=VMEM_LIMIT),
        cost_estimate=pl.CostEstimate(
            flops=slots * BLK * BLK * channels * 4, bytes_accessed=16_000_000, transcendentals=0
        ),
    )(rows, cols, count, vals, grad_rows)


def local(
    acc_feats,
    content_feats,
    block_values,
    block_rows,
    block_cols,
    block_count,
    w_self,
    w_neigh,
    out_grad,
):
    vals = block_values[0, 0]
    rows = block_rows[0, 0]
    cols = block_cols[0, 0]
    count = block_count[0]
    accounts = acc_feats.shape[0]
    chunks = lax.axis_size("col")

    source = lax.all_gather(content_feats.T, "row", axis=0, tiled=True)
    partial = forward_tiles(vals, rows, cols, count, source, chunks)
    summed = lax.psum_scatter(partial, "col", scatter_dimension=0, tiled=True)[0]
    degree = summed[accounts].reshape(-1)[:accounts]
    inv_degree = lax.rsqrt(1.0 + degree)[:, None]
    neigh = summed[:accounts] * inv_degree
    pre_act = jnp.dot(acc_feats, w_self, precision=high) + jnp.dot(neigh, w_neigh, precision=high)
    sigmoid_pre = jax.nn.sigmoid(pre_act)
    activation = pre_act * sigmoid_pre
    inv_rms = lax.rsqrt(jnp.mean(activation * activation, axis=1, keepdims=True) + rms_epsilon)
    layer_out = activation * inv_rms
    d_act = (out_grad - layer_out * jnp.mean(out_grad * layer_out, axis=1, keepdims=True)) * inv_rms
    d_pre = d_act * sigmoid_pre * (1.0 + pre_act * (1.0 - sigmoid_pre))
    d_gathered = jnp.dot(d_pre, w_neigh.T, precision=high) * inv_degree
    grad_rows = lax.all_gather(d_gathered, "col", axis=0, tiled=True)
    back_part = backward_tiles(vals, rows, cols, count, grad_rows)
    grad_content = lax.psum_scatter(back_part, "row", scatter_dimension=0, tiled=True).T
    grad_acc = jnp.dot(d_pre, w_self.T, precision=high)
    acc_total = accounts * lax.axis_size("row") * lax.axis_size("col")
    norm_factor = 1.0 / math.sqrt(acc_total)
    both = jnp.concatenate([acc_feats, neigh], axis=1)
    weight_term = lax.dot_general(both, d_pre, (((0,), (0,)), ((), ())), precision=high)
    weight_grads = lax.psum(weight_term * norm_factor, ("row", "col"))
    features = acc_feats.shape[1]
    return (layer_out, grad_acc, grad_content, weight_grads[:features], weight_grads[features:])


def solution(mesh):
    in_specs = (
        P(("row", "col"), None),
        P("col", "row"),
        P("row", "col", None, None, None),
        P("row", "col", None),
        P("row", "col", None),
        P("row", "col"),
        P(),
        P(),
        P(("row", "col"), None),
    )
    out_specs = (P(("row", "col"), None), P(("row", "col"), None), P("col", "row"), P(), P())
    return jax.shard_map(local, mesh=mesh, in_specs=in_specs, out_specs=out_specs, check_vma=False)
```

```python
import functools
import math

import jax
import jax.numpy as jnp
from jax import lax
from jax.experimental import pallas as pl
from jax.experimental.pallas import tpu as pltpu
from jax.sharding import PartitionSpec as P

BLK = 128
BR = 16
BC = 16
GROUP = 8
PAD = 8
VMEM_LIMIT = 48 * 1024 * 1024
high = lax.Precision.HIGH
rms_epsilon = 1e-05


def split(x):
    hi = x.astype(jnp.bfloat16)
    lo = (x - hi.astype(jnp.float32)).astype(jnp.bfloat16)
    return hi, lo


def forward_kernel(per_chunk, rows_ref, cols_ref, count_ref, vals_ref, source_ref, out_ref, xs, degs):
    step = pl.program_id(0)
    chunks, chunk_rows, _ = out_ref.shape

    @pl.when(step == 0)
    def _():
        for block in range(BC):
            hi, lo = split(source_ref[:, block * BLK : (block + 1) * BLK].T)
            xs[block, 0:BLK, :] = hi
            xs[block, BLK:, :] = lo
        out_ref[...] = jnp.zeros_like(out_ref)
        degs[...] = jnp.zeros_like(degs)

    ones = jnp.ones((8, 2 * BLK), jnp.bfloat16)
    for k in range(GROUP):
        slot = step * GROUP + k

        @pl.when(slot < count_ref[0])
        def _():
            row, col = rows_ref[slot], cols_ref[slot]
            hi, lo = split(vals_ref[k])
            left = jnp.concatenate(
                [jnp.concatenate([hi, hi], axis=1), jnp.concatenate([lo, lo], axis=1)], axis=0
            )
            product = jnp.dot(left, xs[col], preferred_element_type=jnp.float32)
            chunk = row // per_chunk
            begin = pl.multiple_of((row - chunk * per_chunk) * BLK, BLK)
            out_ref[chunk, pl.ds(begin, BLK), :] += product[:BLK] + product[BLK:]
            degs[row] += lax.dot_general(
                ones,
                jnp.concatenate([hi, lo], axis=1),
                (((1,), (1,)), ((), ())),
                preferred_element_type=jnp.float32,
            )

    @pl.when(step == pl.num_programs(0) - 1)
    def _():
        for row in range(BR):
            chunk, place = row // per_chunk, row % per_chunk
            out_ref[chunk, chunk_rows - PAD :, place * BLK : (place + 1) * BLK] = degs[row]


def backward_kernel(rows_ref, cols_ref, count_ref, vals_ref, grad_ref, out_ref, gs):
    step = pl.program_id(0)

    @pl.when(step == 0)
    def _():
        for block in range(BR):
            hi, lo = split(grad_ref[block * BLK : (block + 1) * BLK, :].T)
            gs[block, :, 0:BLK] = hi
            gs[block, :, BLK:] = lo
        out_ref[...] = jnp.zeros_like(out_ref)

    for k in range(GROUP):
        slot = step * GROUP + k

        @pl.when(slot < count_ref[0])
        def _():
            row, col = rows_ref[slot], cols_ref[slot]
            hi, lo = split(vals_ref[k])
            both = jnp.concatenate([hi, lo], axis=1)
            right = jnp.concatenate([both, both], axis=0)
            product = jnp.dot(gs[row], right, preferred_element_type=jnp.float32)
            begin = pl.multiple_of(col * BLK, BLK)
            out_ref[:, pl.ds(begin, BLK)] += product[:, :BLK] + product[:, BLK:]


MESH = pl.DeviceIdType.MESH


def place_of(index, size):
    upper, lower = index // 2, index % 2
    return upper + lower * (size - 1 - 2 * upper)


def index_of(place, size):
    lower = place // (size // 2)
    upper = place + lower * (size - 1 - 2 * place)
    return upper * 2 + lower


def greet(partners):
    barrier = pltpu.get_barrier_semaphore()
    for partner in partners:
        pl.semaphore_signal(barrier, inc=1, device_id=partner, device_id_type=MESH)
    pl.semaphore_wait(barrier, len(partners))


def gather_kernel(size, x_ref, out_ref, send_sems, recv_sems):
    row = lax.axis_index("row")
    col = lax.axis_index("col")
    place = place_of(row, size)
    right = (index_of((place + 1) % size, size), col)
    left = (index_of((place + size - 1) % size, size), col)
    half = x_ref.shape[0] // 2
    greet((left, right))
    out_ref[row] = x_ref[...]
    copies = []
    for step in range(size - 1):
        now = []
        for way, (partner, owner) in enumerate(
            ((right, place + size - step), (left, place + step))
        ):
            block = out_ref.at[index_of(owner % size, size), pl.ds(way * half, half)]
            copy = pltpu.make_async_remote_copy(
                src_ref=block,
                dst_ref=block,
                send_sem=send_sems.at[way, step],
                recv_sem=recv_sems.at[way, step],
                device_id=partner,
                device_id_type=MESH,
            )
            copy.start()
            now.append(copy)
        for copy in now:
            copy.wait_recv()
        copies += now
    for copy in copies:
        copy.wait_send()


def gather_rows(x):
    size = lax.axis_size("row")
    out = pl.pallas_call(
        functools.partial(gather_kernel, size),
        out_shape=jax.ShapeDtypeStruct((size, *x.shape), x.dtype),
        in_specs=[pl.BlockSpec(memory_space=pltpu.VMEM)],
        out_specs=pl.BlockSpec(memory_space=pltpu.VMEM),
        scratch_shapes=[
            pltpu.SemaphoreType.DMA((2, size - 1)),
            pltpu.SemaphoreType.DMA((2, size - 1)),
        ],
        compiler_params=pltpu.CompilerParams(
            collective_id=0, has_side_effects=True, vmem_limit_bytes=VMEM_LIMIT
        ),
    )(x)
    return out.reshape(size * x.shape[0], x.shape[1])


def partners_of(sizes):
    here = [lax.axis_index("row"), lax.axis_index("col")]
    found = []
    for axis in (1, 0):
        reach = 1
        while reach < sizes[axis]:
            bit = (here[axis] // reach) % 2
            there = list(here)
            there[axis] = here[axis] + (1 - 2 * bit) * reach
            found.append((bit, tuple(there)))
            reach *= 2
    return found


def sum_kernel(sizes, x_ref, out_ref, acc, landing, send_sems, recv_sems):
    partners = partners_of(sizes)
    greet([partner for _, partner in partners])
    acc[...] = x_ref[...]
    begin = 0
    length = x_ref.shape[0]
    offset = 0
    begins = []
    for stage, (bit, partner) in enumerate(partners):
        length //= 2
        keep = begin + bit * length
        give = begin + (1 - bit) * length
        copy = pltpu.make_async_remote_copy(
            src_ref=acc.at[pl.ds(pl.multiple_of(give, 8), length)],
            dst_ref=landing.at[pl.ds(offset, length)],
            send_sem=send_sems.at[0, stage],
            recv_sem=recv_sems.at[0, stage],
            device_id=partner,
            device_id_type=MESH,
        )
        copy.start()
        copy.wait()
        keep = pl.multiple_of(keep, 8)
        acc[pl.ds(keep, length), :] += landing[offset : offset + length, :]
        offset += length
        begins.append(begin)
        begin = keep
    out_ref[pl.ds(begin, length), :] = acc[pl.ds(begin, length), :]
    for stage in reversed(range(len(partners))):
        block = out_ref.at[pl.ds(pl.multiple_of(begin, 8), length)]
        copy = pltpu.make_async_remote_copy(
            src_ref=block,
            dst_ref=block,
            send_sem=send_sems.at[1, stage],
            recv_sem=recv_sems.at[1, stage],
            device_id=partners[stage][1],
            device_id_type=MESH,
        )
        copy.start()
        copy.wait()
        begin = begins[stage]
        length *= 2


def sum_all(x):
    sizes = (lax.axis_size("row"), lax.axis_size("col"))
    stages = sum(size.bit_length() - 1 for size in sizes)
    return pl.pallas_call(
        functools.partial(sum_kernel, sizes),
        out_shape=jax.ShapeDtypeStruct(x.shape, x.dtype),
        in_specs=[pl.BlockSpec(memory_space=pltpu.VMEM)],
        out_specs=pl.BlockSpec(memory_space=pltpu.VMEM),
        scratch_shapes=[
            pltpu.VMEM(x.shape, x.dtype),
            pltpu.VMEM(x.shape, x.dtype),
            pltpu.SemaphoreType.DMA((2, stages)),
            pltpu.SemaphoreType.DMA((2, stages)),
        ],
        compiler_params=pltpu.CompilerParams(
            collective_id=1, has_side_effects=True, vmem_limit_bytes=VMEM_LIMIT
        ),
        cost_estimate=pl.CostEstimate(flops=0, bytes_accessed=200_000_000, transcendentals=0),
    )(x)


def values_index(step, rows_ref, cols_ref, count_ref):
    return (jnp.minimum(step, (count_ref[0] - 1) // GROUP), 0, 0)


def whole(*shape):
    return pl.BlockSpec(shape, lambda step, *_: (0,) * len(shape))


def forward_tiles(vals, rows, cols, count, source, chunks):
    channels = source.shape[0]
    per_chunk = BR // chunks
    chunk_rows = per_chunk * BLK + PAD
    slots = vals.shape[0]
    return pl.pallas_call(
        functools.partial(forward_kernel, per_chunk),
        out_shape=jax.ShapeDtypeStruct((chunks, chunk_rows, channels), jnp.float32),
        grid_spec=pltpu.PrefetchScalarGridSpec(
            num_scalar_prefetch=3,
            grid=(slots // GROUP,),
            in_specs=[
                pl.BlockSpec((GROUP, BLK, BLK), values_index),
                whole(channels, BC * BLK),
            ],
            out_specs=whole(chunks, chunk_rows, channels),
            scratch_shapes=[
                pltpu.VMEM((BC, 2 * BLK, channels), jnp.bfloat16),
                pltpu.VMEM((BR, 8, BLK), jnp.float32),
            ],
        ),
        compiler_params=pltpu.CompilerParams(vmem_limit_bytes=VMEM_LIMIT),
        cost_estimate=pl.CostEstimate(
            flops=slots * BLK * BLK * channels * 4, bytes_accessed=16_000_000, transcendentals=0
        ),
    )(rows, cols, count, vals, source)


def backward_tiles(vals, rows, cols, count, grad_rows):
    channels = grad_rows.shape[1]
    slots = vals.shape[0]
    return pl.pallas_call(
        backward_kernel,
        out_shape=jax.ShapeDtypeStruct((channels, BC * BLK), jnp.float32),
        grid_spec=pltpu.PrefetchScalarGridSpec(
            num_scalar_prefetch=3,
            grid=(slots // GROUP,),
            in_specs=[
                pl.BlockSpec((GROUP, BLK, BLK), values_index),
                whole(BR * BLK, channels),
            ],
            out_specs=whole(channels, BC * BLK),
            scratch_shapes=[pltpu.VMEM((BR, channels, 2 * BLK), jnp.bfloat16)],
        ),
        compiler_params=pltpu.CompilerParams(vmem_limit_bytes=VMEM_LIMIT),
        cost_estimate=pl.CostEstimate(
            flops=slots * BLK * BLK * channels * 4, bytes_accessed=16_000_000, transcendentals=0
        ),
    )(rows, cols, count, vals, grad_rows)


def local(
    acc_feats,
    content_feats,
    block_values,
    block_rows,
    block_cols,
    block_count,
    w_self,
    w_neigh,
    out_grad,
):
    vals = block_values[0, 0]
    rows = block_rows[0, 0]
    cols = block_cols[0, 0]
    count = block_count[0]
    accounts = acc_feats.shape[0]
    chunks = lax.axis_size("col")

    source = gather_rows(content_feats.T)
    partial = forward_tiles(vals, rows, cols, count, source, chunks)
    summed = lax.psum_scatter(partial, "col", scatter_dimension=0, tiled=True)[0]
    degree = summed[accounts].reshape(-1)[:accounts]
    inv_degree = lax.rsqrt(1.0 + degree)[:, None]
    neigh = summed[:accounts] * inv_degree
    pre_act = jnp.dot(acc_feats, w_self, precision=high) + jnp.dot(neigh, w_neigh, precision=high)
    sigmoid_pre = jax.nn.sigmoid(pre_act)
    activation = pre_act * sigmoid_pre
    inv_rms = lax.rsqrt(jnp.mean(activation * activation, axis=1, keepdims=True) + rms_epsilon)
    layer_out = activation * inv_rms
    d_act = (out_grad - layer_out * jnp.mean(out_grad * layer_out, axis=1, keepdims=True)) * inv_rms
    d_pre = d_act * sigmoid_pre * (1.0 + pre_act * (1.0 - sigmoid_pre))
    d_gathered = jnp.dot(d_pre, w_neigh.T, precision=high) * inv_degree
    grad_rows = lax.all_gather(d_gathered, "col", axis=0, tiled=True)
    back_part = backward_tiles(vals, rows, cols, count, grad_rows)
    grad_content = lax.psum_scatter(back_part, "row", scatter_dimension=0, tiled=True).T
    grad_acc = jnp.dot(d_pre, w_self.T, precision=high)
    acc_total = accounts * lax.axis_size("row") * lax.axis_size("col")
    norm_factor = 1.0 / math.sqrt(acc_total)
    both = jnp.concatenate([acc_feats, neigh], axis=1)
    weight_term = lax.dot_general(both, d_pre, (((0,), (0,)), ((), ())), precision=high)
    weight_grads = sum_all(weight_term * norm_factor)
    features = acc_feats.shape[1]
    return (layer_out, grad_acc, grad_content, weight_grads[:features], weight_grads[features:])


def solution(mesh):
    in_specs = (
        P(("row", "col"), None),
        P("col", "row"),
        P("row", "col", None, None, None),
        P("row", "col", None),
        P("row", "col", None),
        P("row", "col"),
        P(),
        P(),
        P(("row", "col"), None),
    )
    out_specs = (P(("row", "col"), None), P(("row", "col"), None), P("col", "row"), P(), P())
    return jax.shard_map(local, mesh=mesh, in_specs=in_specs, out_specs=out_specs, check_vma=False)
```

```python
import functools
import math

import jax
import jax.numpy as jnp
from jax import lax
from jax.experimental import pallas as pl
from jax.experimental.pallas import tpu as pltpu
from jax.sharding import PartitionSpec as P

BLK = 128
BR = 16
BC = 16
GROUP = 8
PAD = 8
VMEM_LIMIT = 48 * 1024 * 1024
high = lax.Precision.HIGH
rms_epsilon = 1e-05


def split(x):
    hi = x.astype(jnp.bfloat16)
    lo = (x - hi.astype(jnp.float32)).astype(jnp.bfloat16)
    return hi, lo


def forward_kernel(per_chunk, rows_ref, cols_ref, count_ref, vals_ref, source_ref, out_ref, xs, degs):
    step = pl.program_id(0)
    chunks, chunk_rows, _ = out_ref.shape

    @pl.when(step == 0)
    def _():
        for block in range(BC):
            hi, lo = split(source_ref[:, block * BLK : (block + 1) * BLK].T)
            xs[block, 0:BLK, :] = hi
            xs[block, BLK:, :] = lo
        out_ref[...] = jnp.zeros_like(out_ref)
        degs[...] = jnp.zeros_like(degs)

    ones = jnp.ones((8, 2 * BLK), jnp.bfloat16)
    for k in range(GROUP):
        slot = step * GROUP + k

        @pl.when(slot < count_ref[0])
        def _():
            row, col = rows_ref[slot], cols_ref[slot]
            hi, lo = split(vals_ref[k])
            left = jnp.concatenate(
                [jnp.concatenate([hi, hi], axis=1), jnp.concatenate([lo, lo], axis=1)], axis=0
            )
            product = jnp.dot(left, xs[col], preferred_element_type=jnp.float32)
            chunk = row // per_chunk
            begin = pl.multiple_of((row - chunk * per_chunk) * BLK, BLK)
            out_ref[reversed_bits(chunk, chunks), pl.ds(begin, BLK), :] += product[:BLK] + product[BLK:]
            degs[row] += lax.dot_general(
                ones,
                jnp.concatenate([hi, lo], axis=1),
                (((1,), (1,)), ((), ())),
                preferred_element_type=jnp.float32,
            )

    @pl.when(step == pl.num_programs(0) - 1)
    def _():
        for row in range(BR):
            chunk, place = row // per_chunk, row % per_chunk
            turned = reversed_bits(chunk, chunks)
            out_ref[turned, chunk_rows - PAD :, place * BLK : (place + 1) * BLK] = degs[row]


def backward_kernel(rows_ref, cols_ref, count_ref, vals_ref, grad_ref, out_ref, gs):
    step = pl.program_id(0)

    @pl.when(step == 0)
    def _():
        for block in range(BR):
            hi, lo = split(grad_ref[block * BLK : (block + 1) * BLK, :].T)
            gs[block, :, 0:BLK] = hi
            gs[block, :, BLK:] = lo
        out_ref[...] = jnp.zeros_like(out_ref)

    for k in range(GROUP):
        slot = step * GROUP + k

        @pl.when(slot < count_ref[0])
        def _():
            row, col = rows_ref[slot], cols_ref[slot]
            hi, lo = split(vals_ref[k])
            both = jnp.concatenate([hi, lo], axis=1)
            right = jnp.concatenate([both, both], axis=0)
            product = jnp.dot(gs[row], right, preferred_element_type=jnp.float32)
            begin = pl.multiple_of(col * BLK, BLK)
            out_ref[:, pl.ds(begin, BLK)] += product[:, :BLK] + product[:, BLK:]


MESH = pl.DeviceIdType.MESH


def place_of(index, size):
    upper, lower = index // 2, index % 2
    return upper + lower * (size - 1 - 2 * upper)


def index_of(place, size):
    lower = place // (size // 2)
    upper = place + lower * (size - 1 - 2 * place)
    return upper * 2 + lower


def greet(partners):
    barrier = pltpu.get_barrier_semaphore()
    for partner in partners:
        pl.semaphore_signal(barrier, inc=1, device_id=partner, device_id_type=MESH)
    pl.semaphore_wait(barrier, len(partners))


def gather_kernel(size, x_ref, out_ref, send_sems, recv_sems):
    row = lax.axis_index("row")
    col = lax.axis_index("col")
    place = place_of(row, size)
    right = (index_of((place + 1) % size, size), col)
    left = (index_of((place + size - 1) % size, size), col)
    half = x_ref.shape[0] // 2
    greet((left, right))
    out_ref[row] = x_ref[...]
    copies = []
    for step in range(size - 1):
        now = []
        for way, (partner, owner) in enumerate(
            ((right, place + size - step), (left, place + step))
        ):
            block = out_ref.at[index_of(owner % size, size), pl.ds(way * half, half)]
            copy = pltpu.make_async_remote_copy(
                src_ref=block,
                dst_ref=block,
                send_sem=send_sems.at[way, step],
                recv_sem=recv_sems.at[way, step],
                device_id=partner,
                device_id_type=MESH,
            )
            copy.start()
            now.append(copy)
        for copy in now:
            copy.wait_recv()
        copies += now
    for copy in copies:
        copy.wait_send()


def gather_rows(x):
    size = lax.axis_size("row")
    out = pl.pallas_call(
        functools.partial(gather_kernel, size),
        out_shape=jax.ShapeDtypeStruct((size, *x.shape), x.dtype),
        in_specs=[pl.BlockSpec(memory_space=pltpu.VMEM)],
        out_specs=pl.BlockSpec(memory_space=pltpu.VMEM),
        scratch_shapes=[
            pltpu.SemaphoreType.DMA((2, size - 1)),
            pltpu.SemaphoreType.DMA((2, size - 1)),
        ],
        compiler_params=pltpu.CompilerParams(
            collective_id=0, has_side_effects=True, vmem_limit_bytes=VMEM_LIMIT
        ),
    )(x)
    return out.reshape(size * x.shape[0], x.shape[1])


def partners_of(sizes):
    here = [lax.axis_index("row"), lax.axis_index("col")]
    found = []
    for axis in (1, 0):
        reach = 1
        while reach < sizes[axis]:
            bit = (here[axis] // reach) % 2
            there = list(here)
            there[axis] = here[axis] + (1 - 2 * bit) * reach
            found.append((bit, tuple(there)))
            reach *= 2
    return found


def scatter_kernel(size, x_ref, out_ref, acc, landing, send_sems, recv_sems):
    stages = size.bit_length() - 1
    partners = partners_of((1, size))
    greet([partner for _, partner in partners])
    begin = 0
    length = size
    offset = 0
    for stage, (bit, partner) in enumerate(partners):
        length //= 2
        source = x_ref if stage == 0 else acc
        keep = begin + bit * length
        give = begin + (1 - bit) * length
        copy = pltpu.make_async_remote_copy(
            src_ref=source.at[pl.ds(give, length)],
            dst_ref=landing.at[pl.ds(offset, length)],
            send_sem=send_sems.at[stage],
            recv_sem=recv_sems.at[stage],
            device_id=partner,
            device_id_type=MESH,
        )
        copy.start()
        copy.wait()
        total = source[pl.ds(keep, length)] + landing[offset : offset + length]
        if stage == stages - 1:
            out_ref[...] = total
        else:
            acc[pl.ds(keep, length)] = total
        offset += length
        begin = keep


def scatter_cols(x):
    size = x.shape[0]
    stages = size.bit_length() - 1
    return pl.pallas_call(
        functools.partial(scatter_kernel, size),
        out_shape=jax.ShapeDtypeStruct((1, *x.shape[1:]), x.dtype),
        in_specs=[pl.BlockSpec(memory_space=pltpu.VMEM)],
        out_specs=pl.BlockSpec(memory_space=pltpu.VMEM),
        scratch_shapes=[
            pltpu.VMEM(x.shape, x.dtype),
            pltpu.VMEM(x.shape, x.dtype),
            pltpu.SemaphoreType.DMA((stages,)),
            pltpu.SemaphoreType.DMA((stages,)),
        ],
        compiler_params=pltpu.CompilerParams(
            collective_id=2, has_side_effects=True, vmem_limit_bytes=VMEM_LIMIT
        ),
    )(x)


def sum_kernel(
    sizes, x_ref, parts_ref, out_ref, part_ref, acc, landing, slots, send_sems, recv_sems, ring_send, ring_recv
):
    size = sizes[0]
    row = lax.axis_index("row")
    col = lax.axis_index("col")
    place = place_of(row, size)
    right = (index_of((place + 1) % size, size), col)
    left = (index_of((place + size - 1) % size, size), col)
    half = part_ref.shape[0] // 2
    partners = partners_of(sizes)
    greet([partner for _, partner in partners] + [left, right])
    ring = []

    def ring_copy(step, way):
        partner = (right, left)[way]
        first = index_of((place + (size - 1, 1)[way]) % size, size)
        source = parts_ref.at[first, pl.ds(way * half, half)] if step == 0 else slots.at[way, step - 1]
        copy = pltpu.make_async_remote_copy(
            src_ref=source,
            dst_ref=slots.at[way, step],
            send_sem=ring_send.at[way, step],
            recv_sem=ring_recv.at[way, step],
            device_id=partner,
            device_id_type=MESH,
        )
        copy.start()
        return copy

    def ring_step():
        step = len(ring) // 2 - 1
        for way in range(2):
            ring[2 * step + way].wait_recv()
            owner = (place + (2 * size - 2 - step, 2 + step)[way]) % size
            term = parts_ref[index_of(owner, size), pl.ds(way * half, half), :]
            if step == size - 2:
                part_ref[way * half : (way + 1) * half, :] = slots[way, step] + term
            else:
                slots[way, step] += term
                ring.append(ring_copy(step + 1, way))

    ring += [ring_copy(0, 0), ring_copy(0, 1)]
    done = 0
    acc[...] = x_ref[...]
    begin = 0
    length = x_ref.shape[0]
    offset = 0
    begins = []
    for stage, (bit, partner) in enumerate(partners):
        length //= 2
        keep = begin + bit * length
        give = begin + (1 - bit) * length
        copy = pltpu.make_async_remote_copy(
            src_ref=acc.at[pl.ds(pl.multiple_of(give, 8), length)],
            dst_ref=landing.at[pl.ds(offset, length)],
            send_sem=send_sems.at[0, stage],
            recv_sem=recv_sems.at[0, stage],
            device_id=partner,
            device_id_type=MESH,
        )
        copy.start()
        for _ in range(2 if stage == 1 else 1):
            if done < size - 1:
                ring_step()
                done += 1
        copy.wait()
        keep = pl.multiple_of(keep, 8)
        acc[pl.ds(keep, length), :] += landing[offset : offset + length, :]
        offset += length
        begins.append(begin)
        begin = keep
    out_ref[pl.ds(begin, length), :] = acc[pl.ds(begin, length), :]
    for stage in reversed(range(len(partners))):
        block = out_ref.at[pl.ds(pl.multiple_of(begin, 8), length)]
        copy = pltpu.make_async_remote_copy(
            src_ref=block,
            dst_ref=block,
            send_sem=send_sems.at[1, stage],
            recv_sem=recv_sems.at[1, stage],
            device_id=partners[stage][1],
            device_id_type=MESH,
        )
        copy.start()
        if done < size - 1:
            ring_step()
            done += 1
        copy.wait()
        begin = begins[stage]
        length *= 2
    while done < size - 1:
        ring_step()
        done += 1
    for copy in ring:
        copy.wait_send()


def sum_all(x, parts):
    sizes = (lax.axis_size("row"), lax.axis_size("col"))
    stages = sum(size.bit_length() - 1 for size in sizes)
    size = sizes[0]
    channels, nodes = parts.shape
    channels //= size
    vmem = pl.BlockSpec(memory_space=pltpu.VMEM)
    return pl.pallas_call(
        functools.partial(sum_kernel, sizes),
        out_shape=(
            jax.ShapeDtypeStruct(x.shape, x.dtype),
            jax.ShapeDtypeStruct((channels, nodes), x.dtype),
        ),
        in_specs=[vmem, vmem],
        out_specs=(vmem, vmem),
        scratch_shapes=[
            pltpu.VMEM(x.shape, x.dtype),
            pltpu.VMEM(x.shape, x.dtype),
            pltpu.VMEM((2, size - 1, channels // 2, nodes), x.dtype),
            pltpu.SemaphoreType.DMA((2, stages)),
            pltpu.SemaphoreType.DMA((2, stages)),
            pltpu.SemaphoreType.DMA((2, size - 1)),
            pltpu.SemaphoreType.DMA((2, size - 1)),
        ],
        compiler_params=pltpu.CompilerParams(
            collective_id=1, has_side_effects=True, vmem_limit_bytes=VMEM_LIMIT
        ),
    )(x, parts.reshape(size, channels, nodes))


def reversed_bits(index, size):
    result = 0
    while size > 1:
        result = result * 2 + index % 2
        index = index // 2
        size //= 2
    return result


def values_index(step, rows_ref, cols_ref, count_ref):
    return (jnp.minimum(step, (count_ref[0] - 1) // GROUP), 0, 0)


def whole(*shape):
    return pl.BlockSpec(shape, lambda step, *_: (0,) * len(shape))


def forward_tiles(vals, rows, cols, count, source, chunks):
    channels = source.shape[0]
    per_chunk = BR // chunks
    chunk_rows = per_chunk * BLK + PAD
    slots = vals.shape[0]
    return pl.pallas_call(
        functools.partial(forward_kernel, per_chunk),
        out_shape=jax.ShapeDtypeStruct((chunks, chunk_rows, channels), jnp.float32),
        grid_spec=pltpu.PrefetchScalarGridSpec(
            num_scalar_prefetch=3,
            grid=(slots // GROUP,),
            in_specs=[
                pl.BlockSpec((GROUP, BLK, BLK), values_index),
                whole(channels, BC * BLK),
            ],
            out_specs=whole(chunks, chunk_rows, channels),
            scratch_shapes=[
                pltpu.VMEM((BC, 2 * BLK, channels), jnp.bfloat16),
                pltpu.VMEM((BR, 8, BLK), jnp.float32),
            ],
        ),
        compiler_params=pltpu.CompilerParams(vmem_limit_bytes=VMEM_LIMIT),
        cost_estimate=pl.CostEstimate(
            flops=slots * BLK * BLK * channels * 4, bytes_accessed=16_000_000, transcendentals=0
        ),
    )(rows, cols, count, vals, source)


def backward_tiles(vals, rows, cols, count, grad_rows):
    channels = grad_rows.shape[1]
    slots = vals.shape[0]
    return pl.pallas_call(
        backward_kernel,
        out_shape=jax.ShapeDtypeStruct((channels, BC * BLK), jnp.float32),
        grid_spec=pltpu.PrefetchScalarGridSpec(
            num_scalar_prefetch=3,
            grid=(slots // GROUP,),
            in_specs=[
                pl.BlockSpec((GROUP, BLK, BLK), values_index),
                whole(BR * BLK, channels),
            ],
            out_specs=whole(channels, BC * BLK),
            scratch_shapes=[pltpu.VMEM((BR, channels, 2 * BLK), jnp.bfloat16)],
        ),
        compiler_params=pltpu.CompilerParams(vmem_limit_bytes=VMEM_LIMIT),
        cost_estimate=pl.CostEstimate(
            flops=slots * BLK * BLK * channels * 4, bytes_accessed=16_000_000, transcendentals=0
        ),
    )(rows, cols, count, vals, grad_rows)


def local(
    acc_feats,
    content_feats,
    block_values,
    block_rows,
    block_cols,
    block_count,
    w_self,
    w_neigh,
    out_grad,
):
    vals = block_values[0, 0]
    rows = block_rows[0, 0]
    cols = block_cols[0, 0]
    count = block_count[0]
    accounts = acc_feats.shape[0]
    chunks = lax.axis_size("col")

    source = gather_rows(content_feats.T)
    partial = forward_tiles(vals, rows, cols, count, source, chunks)
    summed = scatter_cols(partial)[0]
    degree = summed[accounts].reshape(-1)[:accounts]
    inv_degree = lax.rsqrt(1.0 + degree)[:, None]
    neigh = summed[:accounts] * inv_degree
    pre_act = jnp.dot(acc_feats, w_self, precision=high) + jnp.dot(neigh, w_neigh, precision=high)
    sigmoid_pre = jax.nn.sigmoid(pre_act)
    activation = pre_act * sigmoid_pre
    inv_rms = lax.rsqrt(jnp.mean(activation * activation, axis=1, keepdims=True) + rms_epsilon)
    layer_out = activation * inv_rms
    d_act = (out_grad - layer_out * jnp.mean(out_grad * layer_out, axis=1, keepdims=True)) * inv_rms
    d_pre = d_act * sigmoid_pre * (1.0 + pre_act * (1.0 - sigmoid_pre))
    d_gathered = jnp.dot(d_pre, w_neigh.T, precision=high) * inv_degree
    grad_rows = lax.all_gather(d_gathered, "col", axis=0, tiled=True)
    grad_acc = jnp.dot(d_pre, w_self.T, precision=high)
    acc_total = accounts * lax.axis_size("row") * lax.axis_size("col")
    norm_factor = 1.0 / math.sqrt(acc_total)
    both = jnp.concatenate([acc_feats, neigh], axis=1)
    weight_term = lax.dot_general(both, d_pre, (((0,), (0,)), ((), ())), precision=high) * norm_factor
    grad_rows, weight_term, grad_acc = lax.optimization_barrier((grad_rows, weight_term, grad_acc))
    back_part = backward_tiles(vals, rows, cols, count, grad_rows)
    weight_grads, grad_content = sum_all(weight_term, back_part)
    grad_content = grad_content.T
    features = acc_feats.shape[1]
    return (layer_out, grad_acc, grad_content, weight_grads[:features], weight_grads[features:])


def solution(mesh):
    in_specs = (
        P(("row", "col"), None),
        P("col", "row"),
        P("row", "col", None, None, None),
        P("row", "col", None),
        P("row", "col", None),
        P("row", "col"),
        P(),
        P(),
        P(("row", "col"), None),
    )
    out_specs = (P(("row", "col"), None), P(("row", "col"), None), P("col", "row"), P(), P())
    return jax.shard_map(local, mesh=mesh, in_specs=in_specs, out_specs=out_specs, check_vma=False)
```
